256 devices in a mesh: dp: 16 (over z_lo, y, core), expert: 16 (over z_hi, x).
Axes of the slice: x: 4, y: 4, z: 8 (z_hi: 4, z_lo: 2; z = z_hi * 2 + z_lo), core: 2. Of those that a mesh axis runs over, the one named last changes fastest.
Arguments:
- quant_rows: bfloat16 [32768, 3584], P(('dp', 'expert')), may hold values from -6 to 6
- row_scales: bfloat16 [32768, 28], P(('dp', 'expert')), may hold values from 0.25 to 4
- out_grad: bfloat16 [32768, 3584], P(('dp', 'expert')), may hold values from -6 to 6
- combine: bfloat16 [32768, 8], P(('dp', 'expert')), may hold values from 0.049804688 to 1
- expert_ids: int32 [32768, 8], P(('dp', 'expert')), may hold values from 0 to 255, all different within a row
- gate_w: bfloat16 [16, 4096, 3584], P('expert', 'dp'), may hold values from -0.09375 to 0.09375
- up_w: bfloat16 [16, 4096, 3584], P('expert', 'dp'), may hold values from -0.09375 to 0.09375
- down_w: bfloat16 [16, 4096, 3584], P('expert', 'dp'), may hold values from -0.125 to 0.125
Outputs:
- in_grad: bfloat16 [32768, 3584], P(('dp', 'expert'))
- combine_grad: bfloat16 [32768, 8], P(('dp', 'expert'))
- gate_w_grad: bfloat16 [16, 4096, 3584], P('expert', 'dp')
- up_w_grad: bfloat16 [16, 4096, 3584], P('expert', 'dp')
- down_w_grad: bfloat16 [16, 4096, 3584], P('expert', 'dp')
The draws below stay inside these ranges and needn't reach their ends.
Inputs may be any that keep to these rules, and one draw needn't show every extreme that they name: `expert_ids`: each row names 8 different experts.
All inputs are finite; a program needn't handle non-finite values.
Results may differ from the reference program's by a relative error of at most 0.02.
Values may be sent and summed in bfloat16 or wider, within the bound.
No kernel may reach another device: no remote copies, remote signals or barrier semaphores. Data moves between devices by JAX's collectives and lax.ppermute only.
A program may use at most 128 MiB of HBM per device.

```python
import math
import jax
import jax.numpy as jnp
from jax import lax

D = 3584
F = 2048
TOPK = 8
EXP_DEV = 16
CAP = 2
TOK_DEV = 128
EXPERTS = 256
HALF_DP = 8
TOKENS = 32768
N_DP = 16
N_EXPERT = 16


def levels(own_key, shape, pieces, smallest, largest):
    def one(axis_at, blocks):
        steps = jax.random.uniform(jax.random.fold_in(jax.random.fold_in(own_key, 6), axis_at), (blocks,), jnp.float32, smallest / len(pieces), largest / len(pieces))
        return jnp.repeat(jnp.exp(steps), shape[axis_at] // blocks).reshape((-1,) + (1,) * (len(shape) - axis_at - 1))

    loudness = one(*pieces[0])
    for cut in pieces[1:]:
        loudness = loudness * one(*cut)
    return loudness


def choose_distinct(own_key, rows, amount, top, lift):
    sequence = jax.random.permutation(jax.random.fold_in(own_key, 1), amount)
    pull = sequence
    for power in range(3):
        pull = pull * pull // amount
    pull = pull * lift // amount
    tickets = jax.random.randint(jax.random.fold_in(own_key, 2), (rows, amount), 0, 4096) + pull
    holders = jax.random.permutation(jax.random.fold_in(own_key, 3), rows)[jnp.arange(amount) % rows]
    tickets = jnp.where(jnp.arange(rows)[:, None] == holders[None, :], 1 << 14, tickets)
    score = tickets * amount + jnp.arange(amount)
    return lax.top_k(score.astype(jnp.int32), top)[1].astype(jnp.int32)


def normal_values(rng, shape, deviation, reach, split=(), kind=jnp.bfloat16):
    result = jax.random.normal(rng, shape, jnp.float32) * deviation
    if len(split) > 0:
        result = levels(rng, shape, split, -0.22, 0.18) * result
    return jnp.clip(result, min=-reach, max=reach).astype(kind)


def setup_inputs(seed: int = 0) -> dict:
    streams_of = jax.random.split(jax.random.key(seed), 9)
    return {
        "quant_rows": normal_values(streams_of[0], (TOKENS, D), 1.0, 6.0, ((0, 256),)),
        "row_scales": jnp.clip(jnp.exp(math.log(4.0) - 2.7725887 * jax.random.uniform(streams_of[1], (TOKENS, D // 128), jnp.float32) ** levels(streams_of[1], (TOKENS, D // 128), ((0, 256),), -0.2, 0.2)), 0.25, 4.0).astype(jnp.bfloat16),
        "out_grad": normal_values(streams_of[2], (TOKENS, D), 1.0, 6.0, ((0, 256),)),
        "combine": jnp.clip(0.049804688 + 0.9501953 * jax.random.uniform(streams_of[3], (TOKENS, TOPK), jnp.float32) ** levels(streams_of[3], (TOKENS, TOPK), ((0, 256),), -0.2, 0.2), 0.049804688, 1.0).astype(jnp.bfloat16),
        "expert_ids": choose_distinct(streams_of[4], TOKENS, EXPERTS, TOPK, 512),
        "gate_w": normal_values(streams_of[5], (N_EXPERT, 2 * F, D), D ** -0.5, 0.09375, ((0, 16), (1, 16))),
        "up_w": normal_values(streams_of[6], (N_EXPERT, 2 * F, D), D ** -0.5, 0.09375, ((0, 16), (1, 16))),
        "down_w": normal_values(streams_of[7], (N_EXPERT, 2 * F, D), F ** -0.5, 0.125, ((0, 16), (1, 16))),
    }


def dequantize(quant_rows, row_scales):
    count_rows = quant_rows.shape[0]
    blocks = quant_rows.astype(jnp.float32).reshape(count_rows, -1, 128) * row_scales.astype(jnp.float32)[:, :, None]
    return blocks.reshape(count_rows, -1).astype(jnp.bfloat16)


def round_blocks(values):
    rounded = lax.optimization_barrier(values.astype(jnp.bfloat16))
    return rounded.astype(jnp.float32)


def reference(quant_rows, row_scales, out_grad, combine, expert_ids, gate_w, up_w, down_w):
    sources = N_DP * N_EXPERT
    window = 2 * N_EXPERT
    slots_all = window * sources * CAP
    hidden_part = F // HALF_DP
    dequant = dequantize(quant_rows, row_scales)
    targets = jnp.arange(window, dtype=jnp.int32) * (EXP_DEV // 2)
    route_hits = (expert_ids.reshape(sources, TOK_DEV * TOPK)[:, :, None] == targets[None, None, :]).astype(jnp.int32)
    route_rank = jnp.cumsum(route_hits, axis=1) - 1
    route_kept = route_hits * (route_rank < CAP).astype(jnp.int32)
    route_live = jnp.sum(route_kept, axis=2) > 0
    expert_of = jnp.sum(route_kept * jnp.arange(window, dtype=jnp.int32)[None, None, :], axis=2)
    rank_of = jnp.sum(route_kept * route_rank, axis=2)
    source_of = jnp.arange(sources, dtype=jnp.int32)[:, None]
    flat_slot = (expert_of * sources + source_of) * CAP + rank_of
    flat_slot = jnp.where(route_live, flat_slot, slots_all).astype(jnp.int32)
    route_index = jnp.arange(sources * TOK_DEV * TOPK, dtype=jnp.int32).reshape(sources, -1)
    table = jnp.zeros((slots_all,), jnp.int32).at[flat_slot.reshape(-1)].set(route_index.reshape(-1) + 1, mode="drop")
    table = table.reshape(window, sources * CAP)
    flat_combine = combine.reshape(-1)
    gate_all = gate_w.reshape(window, F, -1)
    up_all = up_w.reshape(window, F, -1)
    down_all = down_w.reshape(window, F, -1)

    def one_expert(inputs):
        entries, gate_rows, up_rows, down_rows = inputs
        live = entries > 0
        routes = jnp.maximum(entries - 1, 0).astype(jnp.int32)
        tokens = (routes // TOPK).astype(jnp.int32)
        zero_b = jnp.zeros((), jnp.bfloat16)
        rows_x = jnp.where(live[:, None], dequant[tokens], zero_b)
        rows_dy = jnp.where(live[:, None], out_grad[tokens], zero_b)
        weight = jnp.where(live, flat_combine[routes].astype(jnp.float32), jnp.float32(0.0))[:, None]
        h_gate = jnp.dot(rows_x, gate_rows.T, preferred_element_type=jnp.float32)
        h_up = jnp.dot(rows_x, up_rows.T, preferred_element_type=jnp.float32)
        sig = jax.nn.sigmoid(h_gate)
        act = h_gate * sig * h_up
        back = jnp.dot(rows_dy, down_rows.T, preferred_element_type=jnp.float32)
        slot_count = act.shape[0]
        gate_blocks = jnp.sum((act * back).reshape(slot_count, HALF_DP, hidden_part), axis=2)
        gate_value = jnp.sum(round_blocks(gate_blocks), axis=1).astype(jnp.bfloat16)
        scaled = (weight * rows_dy.astype(jnp.float32)).astype(jnp.bfloat16)
        grad_down = jnp.dot(act.astype(jnp.bfloat16).T, scaled, preferred_element_type=jnp.float32)
        d_act = weight * back
        dh_up = (d_act * h_gate * sig).astype(jnp.bfloat16)
        dh_gate = (d_act * h_up * sig * (1.0 + h_gate * (1.0 - sig))).astype(jnp.bfloat16)
        grad_gate = jnp.dot(dh_gate.T, rows_x, preferred_element_type=jnp.float32)
        grad_up = jnp.dot(dh_up.T, rows_x, preferred_element_type=jnp.float32)
        split_gate = dh_gate.astype(jnp.float32).reshape(slot_count, HALF_DP, hidden_part)
        split_up = dh_up.astype(jnp.float32).reshape(slot_count, HALF_DP, hidden_part)
        weights_gate = gate_rows.astype(jnp.float32).reshape(HALF_DP, hidden_part, -1)
        weights_up = up_rows.astype(jnp.float32).reshape(HALF_DP, hidden_part, -1)
        block_terms = jnp.einsum("snf,nfd->snd", split_gate, weights_gate, precision=lax.Precision.HIGHEST)
        block_terms = block_terms + jnp.einsum("snf,nfd->snd", split_up, weights_up, precision=lax.Precision.HIGHEST)
        slot_grad = jnp.sum(round_blocks(block_terms), axis=1).astype(jnp.bfloat16)
        return slot_grad, gate_value, grad_gate.astype(jnp.bfloat16), grad_up.astype(jnp.bfloat16), grad_down.astype(jnp.bfloat16)

    slot_grad, gate_value, gate_grads, up_grads, down_grads = lax.map(one_expert, (table, gate_all, up_all, down_all))
    entries_all = table.reshape(-1)
    live_all = entries_all > 0
    routes_all = jnp.maximum(entries_all - 1, 0).astype(jnp.int32)
    tokens_all = (routes_all // TOPK).astype(jnp.int32)
    slot_rows = jnp.where(live_all[:, None], slot_grad.reshape(-1, slot_grad.shape[-1]).astype(jnp.float32), jnp.float32(0.0))
    in_grad = jnp.zeros((TOKENS, slot_grad.shape[-1]), jnp.float32).at[tokens_all].add(slot_rows).astype(jnp.bfloat16)
    gate_flat = jnp.where(live_all, gate_value.reshape(-1).astype(jnp.float32), jnp.float32(0.0))
    combine_grad = jnp.zeros((TOKENS * TOPK,), jnp.float32).at[routes_all].add(gate_flat)
    combine_grad = combine_grad.astype(jnp.bfloat16).reshape(TOKENS, TOPK)
    gate_w_grad = gate_grads.reshape(N_EXPERT, 2 * F, -1)
    up_w_grad = up_grads.reshape(N_EXPERT, 2 * F, -1)
    down_w_grad = down_grads.reshape(N_EXPERT, 2 * F, -1)
    return in_grad, combine_grad, gate_w_grad, up_w_grad, down_w_grad
```

```python
import jax
import jax.numpy as jnp
from jax import lax
from jax.sharding import Mesh, PartitionSpec as P

EXP_DEV = 16
CAP = 2
SCALE_BLOCK = 128
LANES = 128

rows_pair = (((0,), (0,)), ((), ()))
last_pair = (((1,), (1,)), ((), ()))

COLUMN = ("zlo", "zhi", "x")


def shift_y(value, step):
    count = lax.axis_size("y")
    return lax.ppermute(value, "y", [(i, (i + step) % count) for i in range(count)])


def swap_core(value):
    return lax.ppermute(value, "core", [(0, 1), (1, 0)])


def dequantize(quant_rows, row_scales):
    count_rows = quant_rows.shape[0]
    blocks = (
        quant_rows.astype(jnp.float32).reshape(count_rows, -1, SCALE_BLOCK)
        * row_scales.astype(jnp.float32)[:, :, None]
    )
    return blocks.reshape(count_rows, -1).astype(jnp.bfloat16)


def route(expert_ids, window):
    tok_count, top_count = expert_ids.shape
    slot_total = window * CAP
    column = jnp.arange(slot_total, dtype=jnp.int32)
    group = column // CAP
    rank = column % CAP
    half_window = window // 2
    target = (group % half_window) * EXP_DEV + (group // half_window) * (EXP_DEV // 2)
    hits = [
        (expert_ids[:, k : k + 1] == target[None, :]).astype(jnp.float32)
        for k in range(top_count)
    ]
    hit = sum(hits)
    before = jnp.tril(jnp.ones((tok_count, tok_count), jnp.float32), -1)
    place = jnp.dot(
        before.astype(jnp.bfloat16),
        hit.astype(jnp.bfloat16),
        preferred_element_type=jnp.float32,
    )
    kept = hit * (place == rank[None, :].astype(jnp.float32)).astype(jnp.float32)
    return hits, kept


def body(quant_rows, row_scales, out_grad, combine, expert_ids, gate_w, up_w, down_w):
    top_count = expert_ids.shape[1]
    width = quant_rows.shape[1]
    groups = lax.axis_size("zlo") * lax.axis_size("zhi") * lax.axis_size("x")
    hits, kept = route(expert_ids, groups)
    slots = groups * CAP
    kept_b = kept.astype(jnp.bfloat16)
    rows = dequantize(quant_rows, row_scales)
    weights = combine.astype(jnp.float32)
    slot_weight = sum(hits[k] * weights[:, k : k + 1] for k in range(top_count)) * kept
    slot_weight = jnp.sum(slot_weight, axis=0)
    pick = lambda v: lax.dot_general(
        kept_b, v, rows_pair, preferred_element_type=jnp.float32
    ).astype(jnp.bfloat16)
    tail = jnp.broadcast_to(slot_weight[:, None], (slots, LANES)).astype(jnp.bfloat16)
    send = jnp.concatenate([pick(rows), pick(out_grad), tail], axis=1)
    wide = send.shape[1]
    own = lax.all_to_all(
        send.reshape(groups, CAP, wide), COLUMN, split_axis=0, concat_axis=0, tiled=True
    ).reshape(slots, wide)

    half = slots // 2
    below = shift_y(own, 1)
    above = shift_y(own, -1)
    own_twin = swap_core(own)
    near = jnp.concatenate([below, above], axis=0)
    far_low = shift_y(below[:half], 1)
    far_high = shift_y(above[half:], -1)
    near_twin = swap_core(near)
    far = jnp.concatenate([far_low, far_high], axis=0)
    far_twin = swap_core(far)
    everything = jnp.concatenate(
        [own, near, far, own_twin, near_twin, far_twin], axis=0
    )
    x = everything[:, :width]
    dy = everything[:, width : 2 * width]
    weight = everything[:, 2 * width : 2 * width + 1].astype(jnp.float32)

    gate_rows = gate_w[0]
    up_rows = up_w[0]
    down_rows = down_w[0]
    h_gate = lax.dot_general(x, gate_rows, last_pair, preferred_element_type=jnp.float32)
    h_up = lax.dot_general(x, up_rows, last_pair, preferred_element_type=jnp.float32)
    sig = jax.nn.sigmoid(h_gate)
    act = h_gate * sig * h_up
    back = lax.dot_general(dy, down_rows, last_pair, preferred_element_type=jnp.float32)
    gate_part = jnp.sum(act * back, axis=1)
    scaled = (weight * dy.astype(jnp.float32)).astype(jnp.bfloat16)
    grad_down = lax.dot_general(
        act.astype(jnp.bfloat16), scaled, rows_pair, preferred_element_type=jnp.float32
    )
    d_act = weight * back
    dh_up = (d_act * h_gate * sig).astype(jnp.bfloat16)
    dh_gate = (d_act * h_up * sig * (1.0 + h_gate * (1.0 - sig))).astype(jnp.bfloat16)
    grad_gate = lax.dot_general(dh_gate, x, rows_pair, preferred_element_type=jnp.float32)
    grad_up = lax.dot_general(dh_up, x, rows_pair, preferred_element_type=jnp.float32)
    part = jnp.dot(dh_gate, gate_rows, preferred_element_type=jnp.float32)
    part = part + jnp.dot(dh_up, up_rows, preferred_element_type=jnp.float32)
    part = jnp.concatenate(
        [part, jnp.broadcast_to(gate_part[:, None], (part.shape[0], LANES))], axis=1
    )

    mine, other = part[: 4 * slots], part[4 * slots :]
    mine = mine + swap_core(other.astype(jnp.bfloat16)).astype(jnp.float32)
    s_own, s_below, s_above, s_far = (mine[k * slots : (k + 1) * slots] for k in range(4))
    far_b = s_far.astype(jnp.bfloat16)
    from_below = shift_y(far_b[:half], 1).astype(jnp.float32)
    from_above = shift_y(far_b[half:], -1).astype(jnp.float32)
    to_above = jnp.concatenate([s_above[:half] + from_below, s_above[half:]], axis=0)
    to_below = jnp.concatenate([s_below[:half], s_below[half:] + from_above], axis=0)
    total = (
        s_own
        + shift_y(to_above.astype(jnp.bfloat16), 1).astype(jnp.float32)
        + shift_y(to_below.astype(jnp.bfloat16), -1).astype(jnp.float32)
    ).astype(jnp.bfloat16)
    home = lax.all_to_all(
        total.reshape(groups, CAP, -1), COLUMN, split_axis=0, concat_axis=0, tiled=True
    ).reshape(slots, -1)
    in_grad = jnp.dot(kept_b, home[:, :width], preferred_element_type=jnp.float32).astype(
        jnp.bfloat16
    )
    slot_gate = home[:, width].astype(jnp.float32)[None, :] * kept
    combine_grad = jnp.stack(
        [jnp.sum(hits[k] * slot_gate, axis=1) for k in range(top_count)], axis=1
    ).astype(jnp.bfloat16)
    return (
        in_grad,
        combine_grad,
        grad_gate.astype(jnp.bfloat16)[None],
        grad_up.astype(jnp.bfloat16)[None],
        grad_down.astype(jnp.bfloat16)[None],
    )


def solution(mesh):
    fine = Mesh(
        mesh.devices.reshape(2, 4, 2, 4, 4), ("zlo", "y", "core", "zhi", "x")
    )
    tokens = P(("zlo", "y", "core", "zhi", "x"), None)
    hidden = P(("zhi", "x"), ("zlo", "y", "core"), None)
    return jax.shard_map(
        body,
        mesh=fine,
        in_specs=(tokens,) * 5 + (hidden,) * 3,
        out_specs=(tokens,) * 2 + (hidden,) * 3,
        check_vma=False,
    )
```

```python
import functools

import jax
import jax.numpy as jnp
from jax import lax
from jax.experimental import pallas as pl
from jax.experimental.pallas import tpu as pltpu
from jax.sharding import Mesh, PartitionSpec as P

EXP_DEV = 16
CAP = 2
SCALE_BLOCK = 128
LANES = 128
CHUNK = 512

rows_pair = (((0,), (0,)), ((), ()))
last_pair = (((1,), (1,)), ((), ()))

COLUMN = ("zlo", "zhi", "x")
MIB = 1 << 20
F32 = jnp.float32
BF16 = jnp.bfloat16


def along_y(value, step):
    count = lax.axis_size("y")
    return lax.ppermute(value, "y", [(i, (i + step) % count) for i in range(count)])


def swap_core(value):
    return lax.ppermute(value, "core", [(0, 1), (1, 0)])


def in_hbm(value):
    return pltpu.with_memory_space_constraint(value, pltpu.HBM)


def call(kernel, outs, scratch, vmem, cost, *args, space=pltpu.VMEM, out_space=None):
    flops, moved = cost
    if out_space is None:
        out_shape = [jax.ShapeDtypeStruct(s, t) for s, t in outs]
    else:
        out_shape = [out_space(s, t) for s, t in outs]
    return pl.pallas_call(
        kernel,
        out_shape=out_shape,
        in_specs=[pl.BlockSpec(memory_space=space)] * len(args),
        out_specs=[pl.BlockSpec(memory_space=pltpu.VMEM)] * len(outs),
        scratch_shapes=scratch,
        compiler_params=pltpu.CompilerParams(vmem_limit_bytes=vmem * MIB),
        cost_estimate=pl.CostEstimate(
            flops=flops, bytes_accessed=moved, transcendentals=0
        ),
    )(*args)


def dot(left, right, dims=(((1,), (0,)), ((), ()))):
    return lax.dot_general(left, right, dims, preferred_element_type=F32)


def slot_targets(slots):
    slot = lax.broadcasted_iota(jnp.int32, (slots, 1), 0)
    group = slot // CAP
    half = slots // CAP // 2
    target = (group % half) * EXP_DEV + (group // half) * (EXP_DEV // 2)
    return target, slot % CAP


def fetch_all(sources, local, sems):
    copies = [
        pltpu.make_async_copy(source, target, sems.at[k])
        for k, (source, target) in enumerate(zip(sources, local, strict=True))
    ]
    for copy in copies:
        copy.start()
    return copies


def send_kernel(*refs):
    send_ref, kept_ref, tail_ref = refs[4:7]
    ids_ref, combine_ref, scale_ref, quant_ref = local = refs[7:11]
    copies = fetch_all(refs[:4], local, refs[11])
    top, tokens = ids_ref.shape
    slots = kept_ref.shape[0]
    width = quant_ref.shape[1]
    target, rank = slot_targets(slots)
    row = lax.broadcasted_iota(jnp.int32, (tokens, tokens), 0)
    col = lax.broadcasted_iota(jnp.int32, (tokens, tokens), 1)
    earlier = (row < col).astype(F32).astype(BF16)
    hit = jnp.zeros((slots, tokens), F32)
    weight = jnp.zeros((slots, tokens), F32)
    copies[0].wait()
    copies[1].wait()
    for k in range(top):
        one = ids_ref[k : k + 1, :] == target
        hit = hit + one.astype(F32)
        weight = weight + jnp.where(one, combine_ref[k : k + 1, :].astype(F32), 0.0)
    place = dot(hit.astype(BF16), earlier)
    kept = jnp.where(place == rank.astype(F32), hit, 0.0)
    kept_b = kept.astype(BF16)
    kept_ref[...] = kept_b
    picked = jnp.sum(kept * weight, axis=1, keepdims=True)
    tail_ref[...] = jnp.broadcast_to(picked, tail_ref.shape).astype(BF16)
    copies[2].wait()
    scales = dot(kept_b, scale_ref[...], last_pair)
    copies[3].wait()
    for c in range(0, width, CHUNK):
        rows = dot(kept_b, quant_ref[:, c : c + CHUNK])
        for i in range(0, CHUNK, SCALE_BLOCK):
            b = (c + i) // SCALE_BLOCK
            send_ref[:, c + i : c + i + SCALE_BLOCK] = (
                rows[:, i : i + SCALE_BLOCK] * scales[:, b : b + 1]
            ).astype(BF16)


def pick_kernel(kept_ref, dy_ref, tail_ref, out_ref):
    width = dy_ref.shape[1]
    for c in range(0, width, CHUNK):
        at = pl.ds(c, CHUNK)
        out_ref[:, at] = dot(kept_ref[...], dy_ref[:, at]).astype(BF16)
    out_ref[:, width:] = tail_ref[...]


def home_kernel(home_ref, kept_ref, ids_ref, in_ref, combine_ref):
    width = in_ref.shape[1]
    top, tokens = ids_ref.shape
    slots = kept_ref.shape[0]
    kept = kept_ref[...]
    for c in range(0, width, CHUNK):
        at = pl.ds(c, CHUNK)
        in_ref[:, at] = dot(kept, home_ref[:, at], rows_pair).astype(BF16)
    target, _ = slot_targets(slots)
    value = kept.astype(F32) * home_ref[:, width : width + 1].astype(F32)
    for k in range(top):
        mine = jnp.where(ids_ref[k : k + 1, :] == target, value, 0.0)
        combine_ref[k : k + 1, :] = jnp.sum(mine, axis=0, keepdims=True).astype(BF16)


def body(quant_rows, row_scales, out_grad, combine, expert_ids, gate_w, up_w, down_w):
    top_count = expert_ids.shape[1]
    width = quant_rows.shape[1]
    groups = lax.axis_size("zlo") * lax.axis_size("zhi") * lax.axis_size("x")
    tokens = quant_rows.shape[0]
    units = gate_w.shape[1]
    slots = groups * CAP
    wide = width + LANES
    sources = [in_hbm(v) for v in (expert_ids.T, combine.T, row_scales.T, quant_rows)]
    send_x, kept, tail = call(
        send_kernel,
        [((slots, width), BF16), ((slots, tokens), BF16), ((slots, LANES), BF16)],
        [pltpu.VMEM(v.shape, v.dtype) for v in sources]
        + [pltpu.SemaphoreType.DMA((len(sources),))],
        8,
        (2 * tokens * slots * width, MIB),
        *sources,
        space=pltpu.HBM,
    )
    (send_d,) = call(
        pick_kernel,
        [((slots, wide), BF16)],
        [],
        8,
        (2 * tokens * slots * width, 2 * MIB),
        kept,
        out_grad,
        tail,
    )
    half = slots // 2

    def spread(send):
        wide = send.shape[1]
        own = lax.all_to_all(
            send.reshape(groups, CAP, wide),
            COLUMN,
            split_axis=0,
            concat_axis=0,
            tiled=True,
        ).reshape(slots, wide)
        below = along_y(own, 1)
        above = along_y(own, -1)
        far_low = along_y(below[:half], 1)
        far_high = along_y(above[half:], -1)
        near = jnp.concatenate([own, below, above], axis=0)
        near = jnp.concatenate([near, swap_core(near)], axis=0)
        return near, (far_low, far_high)

    gate_rows = gate_w[0]
    up_rows = up_w[0]
    down_rows = down_w[0]

    def work(x, dy_wide):
        dy = dy_wide[:, :width]
        weight = dy_wide[:, width : width + 1].astype(jnp.float32)
        h_gate = lax.dot_general(
            x, gate_rows, last_pair, preferred_element_type=jnp.float32
        )
        h_up = lax.dot_general(x, up_rows, last_pair, preferred_element_type=jnp.float32)
        sig = jax.nn.sigmoid(h_gate)
        act = h_gate * sig * h_up
        back = lax.dot_general(
            dy, down_rows, last_pair, preferred_element_type=jnp.float32
        )
        gate_part = jnp.sum(act * back, axis=1)
        scaled = (weight * dy.astype(jnp.float32)).astype(jnp.bfloat16)
        d_act = weight * back
        dh_up = (d_act * h_gate * sig).astype(jnp.bfloat16)
        dh_gate = (d_act * h_up * sig * (1.0 + h_gate * (1.0 - sig))).astype(
            jnp.bfloat16
        )
        part = jnp.dot(dh_gate, gate_rows, preferred_element_type=jnp.float32)
        part = part + jnp.dot(dh_up, up_rows, preferred_element_type=jnp.float32)
        part = jnp.concatenate(
            [part, jnp.broadcast_to(gate_part[:, None], (part.shape[0], LANES))], axis=1
        )
        count = part.shape[0] // 2
        mine = part[:count] + swap_core(part[count:].astype(jnp.bfloat16)).astype(
            jnp.float32
        )
        return mine, act.astype(jnp.bfloat16), scaled, dh_gate, dh_up

    near_x, far_x = spread(send_x)
    near_d, far_d = spread(send_d)
    near_sum, near_act, near_scaled, near_gate, near_up = work(near_x, near_d)
    far_x, far_d, _ = lax.optimization_barrier((far_x, far_d, (near_act, near_gate, near_up)))
    far_x, far_d = (jnp.concatenate(v, axis=0) for v in (far_x, far_d))
    far_x, far_d = (jnp.concatenate([v, swap_core(v)], axis=0) for v in (far_x, far_d))
    far_sum, far_act, far_scaled, far_gate, far_up = work(far_x, far_d)

    def weight_grad(a_near, a_far, b_near, b_far):
        return lax.dot_general(
            jnp.concatenate([a_near, a_far], axis=0),
            jnp.concatenate([b_near, b_far], axis=0),
            rows_pair,
            preferred_element_type=jnp.float32,
        )

    grad_gate = weight_grad(near_gate, far_gate, near_x, far_x)
    grad_up = weight_grad(near_up, far_up, near_x, far_x)
    grad_down = weight_grad(near_act, far_act, near_scaled, far_scaled)

    def send_y(value, step):
        return along_y(value.astype(jnp.bfloat16), step).astype(jnp.float32)

    s_own, s_below, s_above = (near_sum[k * slots : (k + 1) * slots] for k in range(3))
    above_low = s_above[:half] + send_y(far_sum[:half], 1)
    below_high = s_below[half:] + send_y(far_sum[half:], -1)
    high = s_own[half:] + send_y(s_above[half:], 1)
    low = s_own[:half] + send_y(s_below[:half], -1)
    low = low + send_y(above_low, 1)
    high = high + send_y(below_high, -1)
    total = jnp.concatenate([low, high], axis=0).astype(jnp.bfloat16)
    home = lax.all_to_all(
        total.reshape(groups, CAP, -1), COLUMN, split_axis=0, concat_axis=0, tiled=True
    ).reshape(slots, -1)
    in_grad, combine_grad = call(
        home_kernel,
        [((tokens, width), BF16), ((top_count, tokens), BF16)],
        [],
        8,
        (2 * tokens * slots * width, 2 * MIB),
        home,
        kept,
        expert_ids.T,
    )
    return (
        in_grad,
        combine_grad.T,
        grad_gate.astype(jnp.bfloat16)[None],
        grad_up.astype(jnp.bfloat16)[None],
        grad_down.astype(jnp.bfloat16)[None],
    )


def solution(mesh):
    fine = Mesh(
        mesh.devices.reshape(2, 4, 2, 4, 4), ("zlo", "y", "core", "zhi", "x")
    )
    tokens = P(("zlo", "y", "core", "zhi", "x"), None)
    hidden = P(("zhi", "x"), ("zlo", "y", "core"), None)
    return jax.shard_map(
        body,
        mesh=fine,
        in_specs=(tokens,) * 5 + (hidden,) * 3,
        out_specs=(tokens,) * 2 + (hidden,) * 3,
        check_vma=False,
    )
```

```python
import functools

import jax
import jax.numpy as jnp
from jax import lax
from jax.experimental import pallas as pl
from jax.experimental.pallas import tpu as pltpu
from jax.sharding import Mesh, PartitionSpec as P

EXP_DEV = 16
CAP = 2
SCALE_BLOCK = 128
LANES = 128
CHUNK = 512

rows_pair = (((0,), (0,)), ((), ()))
last_pair = (((1,), (1,)), ((), ()))

COLUMN = ("zlo", "zhi", "x")
MIB = 1 << 20
F32 = jnp.float32
BF16 = jnp.bfloat16


def along_y(value, step):
    count = lax.axis_size("y")
    return lax.ppermute(value, "y", [(i, (i + step) % count) for i in range(count)])


def swap_core(value):
    return lax.ppermute(value, "core", [(0, 1), (1, 0)])


def in_hbm(value):
    return pltpu.with_memory_space_constraint(value, pltpu.HBM)


def call(kernel, outs, scratch, vmem, cost, *args, space=pltpu.VMEM, out_space=None):
    flops, moved = cost
    if out_space is None:
        out_shape = [jax.ShapeDtypeStruct(s, t) for s, t in outs]
    else:
        out_shape = [out_space(s, t) for s, t in outs]
    return pl.pallas_call(
        kernel,
        out_shape=out_shape,
        in_specs=[pl.BlockSpec(memory_space=space)] * len(args),
        out_specs=[pl.BlockSpec(memory_space=pltpu.VMEM)] * len(outs),
        scratch_shapes=scratch,
        compiler_params=pltpu.CompilerParams(vmem_limit_bytes=vmem * MIB),
        cost_estimate=pl.CostEstimate(
            flops=flops, bytes_accessed=moved, transcendentals=0
        ),
    )(*args)


def dot(left, right, dims=(((1,), (0,)), ((), ()))):
    return lax.dot_general(left, right, dims, preferred_element_type=F32)


def slot_targets(slots):
    slot = lax.broadcasted_iota(jnp.int32, (slots, 1), 0)
    group = slot // CAP
    half = slots // CAP // 2
    target = (group % half) * EXP_DEV + (group // half) * (EXP_DEV // 2)
    return target, slot % CAP


def fetch_all(sources, local, sems):
    copies = [
        pltpu.make_async_copy(source, target, sems.at[k])
        for k, (source, target) in enumerate(zip(sources, local, strict=True))
    ]
    for copy in copies:
        copy.start()
    return copies


def send_kernel(*refs):
    send_ref, kept_ref, tail_ref = refs[4:7]
    ids_ref, combine_ref, scale_ref, quant_ref = local = refs[7:11]
    copies = fetch_all(refs[:4], local, refs[11])
    top, tokens = ids_ref.shape
    slots = kept_ref.shape[0]
    width = quant_ref.shape[1]
    target, rank = slot_targets(slots)
    row = lax.broadcasted_iota(jnp.int32, (tokens, tokens), 0)
    col = lax.broadcasted_iota(jnp.int32, (tokens, tokens), 1)
    earlier = (row < col).astype(F32).astype(BF16)
    hit = jnp.zeros((slots, tokens), F32)
    weight = jnp.zeros((slots, tokens), F32)
    copies[0].wait()
    copies[1].wait()
    for k in range(top):
        one = ids_ref[k : k + 1, :] == target
        hit = hit + one.astype(F32)
        weight = weight + jnp.where(one, combine_ref[k : k + 1, :].astype(F32), 0.0)
    place = dot(hit.astype(BF16), earlier)
    kept = jnp.where(place == rank.astype(F32), hit, 0.0)
    kept_b = kept.astype(BF16)
    kept_ref[...] = kept_b
    picked = jnp.sum(kept * weight, axis=1, keepdims=True)
    tail_ref[...] = jnp.broadcast_to(picked, tail_ref.shape).astype(BF16)
    copies[2].wait()
    scales = dot(kept_b, scale_ref[...], last_pair)
    copies[3].wait()
    for c in range(0, width, CHUNK):
        rows = dot(kept_b, quant_ref[:, c : c + CHUNK])
        for i in range(0, CHUNK, SCALE_BLOCK):
            b = (c + i) // SCALE_BLOCK
            send_ref[:, c + i : c + i + SCALE_BLOCK] = (
                rows[:, i : i + SCALE_BLOCK] * scales[:, b : b + 1]
            ).astype(BF16)


def pick_kernel(kept_ref, dy_ref, tail_ref, out_ref):
    width = dy_ref.shape[1]
    for c in range(0, width, CHUNK):
        at = pl.ds(c, CHUNK)
        out_ref[:, at] = dot(kept_ref[...], dy_ref[:, at]).astype(BF16)
    out_ref[:, width:] = tail_ref[...]


def work_kernel(n_pieces, *refs):
    x_pieces, refs = refs[:n_pieces], refs[n_pieces:]
    pieces = refs[:n_pieces]
    gate_ref, up_ref, down_ref, mine_ref, twin_ref = refs[n_pieces : n_pieces + 5]
    act_ref, dh_gate_ref, dh_up_ref, x_ref, dy_ref = refs[n_pieces + 5 :]
    width = down_ref.shape[2]
    half = mine_ref.shape[0]
    first = 0
    for x_piece, piece in zip(x_pieces, pieces, strict=True):
        at = pl.ds(first, piece.shape[0])
        x_ref[at, :] = x_piece[...]
        dy_ref[at, :] = piece[...]
        first += piece.shape[0]
    h_gate = dot(x_ref[...], gate_ref[0], last_pair)
    h_up = dot(x_ref[...], up_ref[0], last_pair)
    back = dot(dy_ref[:, :width], down_ref[0], last_pair)
    weight = dy_ref[:, width : width + 1].astype(F32)
    sig = jax.nn.sigmoid(h_gate)
    silu = h_gate * sig
    act = silu * h_up
    gate_part = jnp.sum(act * back, axis=1, keepdims=True)
    d_act = weight * back
    act_ref[...] = act.astype(BF16)
    dh_up_ref[...] = (d_act * silu).astype(BF16)
    dh_gate_ref[...] = (d_act * h_up * sig * (1.0 + h_gate * (1.0 - sig))).astype(BF16)
    for c in range(0, width, CHUNK):
        at = pl.ds(c, CHUNK)
        part = dot(dh_gate_ref[...], gate_ref[0, :, at]) + dot(
            dh_up_ref[...], up_ref[0, :, at]
        )
        mine_ref[:, at] = part[:half].astype(BF16)
        twin_ref[:, at] = part[half:].astype(BF16)
    tail = jnp.broadcast_to(gate_part, (2 * half, LANES)).astype(BF16)
    mine_ref[:, width:] = tail[:half]
    twin_ref[:, width:] = tail[half:]


def home_kernel(home_ref, kept_ref, ids_ref, in_ref, combine_ref):
    width = in_ref.shape[1]
    top, tokens = ids_ref.shape
    slots = kept_ref.shape[0]
    kept = kept_ref[...]
    for c in range(0, width, CHUNK):
        at = pl.ds(c, CHUNK)
        in_ref[:, at] = dot(kept, home_ref[:, at], rows_pair).astype(BF16)
    target, _ = slot_targets(slots)
    value = kept.astype(F32) * home_ref[:, width : width + 1].astype(F32)
    for k in range(top):
        mine = jnp.where(ids_ref[k : k + 1, :] == target, value, 0.0)
        combine_ref[k : k + 1, :] = jnp.sum(mine, axis=0, keepdims=True).astype(BF16)


def body(quant_rows, row_scales, out_grad, combine, expert_ids, gate_w, up_w, down_w):
    top_count = expert_ids.shape[1]
    width = quant_rows.shape[1]
    groups = lax.axis_size("zlo") * lax.axis_size("zhi") * lax.axis_size("x")
    tokens = quant_rows.shape[0]
    units = gate_w.shape[1]
    slots = groups * CAP
    wide = width + LANES
    sources = [in_hbm(v) for v in (expert_ids.T, combine.T, row_scales.T, quant_rows)]
    send_x, kept, tail = call(
        send_kernel,
        [((slots, width), BF16), ((slots, tokens), BF16), ((slots, LANES), BF16)],
        [pltpu.VMEM(v.shape, v.dtype) for v in sources]
        + [pltpu.SemaphoreType.DMA((len(sources),))],
        8,
        (2 * tokens * slots * width, MIB),
        *sources,
        space=pltpu.HBM,
    )
    (send_d,) = call(
        pick_kernel,
        [((slots, wide), BF16)],
        [],
        8,
        (2 * tokens * slots * width, 2 * MIB),
        kept,
        out_grad,
        tail,
    )
    half = slots // 2

    def spread(send):
        wide = send.shape[1]
        own = lax.all_to_all(
            send.reshape(groups, CAP, wide),
            COLUMN,
            split_axis=0,
            concat_axis=0,
            tiled=True,
        ).reshape(slots, wide)
        below = along_y(own, 1)
        above = along_y(own, -1)
        far_low = along_y(below[:half], 1)
        far_high = along_y(above[half:], -1)
        near = jnp.concatenate([own, below, above], axis=0)
        near = jnp.concatenate([near, swap_core(near)], axis=0)
        return near, (far_low, far_high)

    gate_rows = gate_w[0]
    up_rows = up_w[0]
    down_rows = down_w[0]

    def work(x, dy_wide):
        dy = dy_wide[:, :width]
        weight = dy_wide[:, width : width + 1].astype(jnp.float32)
        h_gate = lax.dot_general(
            x, gate_rows, last_pair, preferred_element_type=jnp.float32
        )
        h_up = lax.dot_general(x, up_rows, last_pair, preferred_element_type=jnp.float32)
        sig = jax.nn.sigmoid(h_gate)
        act = h_gate * sig * h_up
        back = lax.dot_general(
            dy, down_rows, last_pair, preferred_element_type=jnp.float32
        )
        gate_part = jnp.sum(act * back, axis=1)
        d_act = weight * back
        dh_up = (d_act * h_gate * sig).astype(jnp.bfloat16)
        dh_gate = (d_act * h_up * sig * (1.0 + h_gate * (1.0 - sig))).astype(
            jnp.bfloat16
        )
        part = jnp.dot(dh_gate, gate_rows, preferred_element_type=jnp.float32)
        part = part + jnp.dot(dh_up, up_rows, preferred_element_type=jnp.float32)
        part = jnp.concatenate(
            [part, jnp.broadcast_to(gate_part[:, None], (part.shape[0], LANES))], axis=1
        )
        count = part.shape[0] // 2
        mine = part[:count] + swap_core(part[count:].astype(jnp.bfloat16)).astype(
            jnp.float32
        )
        return mine, act.astype(jnp.bfloat16), dh_gate, dh_up

    near_x, far_x = spread(send_x)
    near_d, far_d = spread(send_d)
    near_sum, near_act, near_gate, near_up = work(near_x, near_d)
    far_x, far_d, _ = lax.optimization_barrier((far_x, far_d, (near_act, near_gate, near_up)))
    far_x, far_d = (jnp.concatenate(v, axis=0) for v in (far_x, far_d))
    far_x, far_d = (jnp.concatenate([v, swap_core(v)], axis=0) for v in (far_x, far_d))
    far_rows = far_x.shape[0]
    far_mine, far_twin, far_act, far_gate, far_up = call(
        functools.partial(work_kernel, 1),
        [((far_rows // 2, wide), BF16)] * 2 + [((far_rows, units), BF16)] * 3,
        [pltpu.VMEM((far_rows, width), BF16), pltpu.VMEM((far_rows, wide), BF16)],
        8,
        (10 * far_rows * width * units, 2 * MIB),
        far_x,
        far_d,
        gate_w,
        up_w,
        down_w,
    )
    far_sum = far_mine.astype(F32) + swap_core(far_twin).astype(F32)

    def send_y(value, step):
        return along_y(value.astype(jnp.bfloat16), step).astype(jnp.float32)

    s_own, s_below, s_above = (near_sum[k * slots : (k + 1) * slots] for k in range(3))
    above_low = s_above[:half] + send_y(far_sum[:half], 1)
    below_high = s_below[half:] + send_y(far_sum[half:], -1)
    high = s_own[half:] + send_y(s_above[half:], 1)
    low = s_own[:half] + send_y(s_below[:half], -1)
    low = low + send_y(above_low, 1)
    high = high + send_y(below_high, -1)
    total = jnp.concatenate([low, high], axis=0).astype(jnp.bfloat16)
    near_d, far_d, _ = lax.optimization_barrier((near_d, far_d, total))
    near_scaled, far_scaled = (
        (v[:, width : width + 1].astype(F32) * v[:, :width].astype(F32)).astype(BF16)
        for v in (near_d, far_d)
    )

    def weight_grad(a_near, a_far, b_near, b_far):
        return lax.dot_general(
            jnp.concatenate([a_near, a_far], axis=0),
            jnp.concatenate([b_near, b_far], axis=0),
            rows_pair,
            preferred_element_type=jnp.float32,
        )

    grad_gate = weight_grad(near_gate, far_gate, near_x, far_x)
    grad_up = weight_grad(near_up, far_up, near_x, far_x)
    grad_down = weight_grad(near_act, far_act, near_scaled, far_scaled)

    home = lax.all_to_all(
        total.reshape(groups, CAP, -1), COLUMN, split_axis=0, concat_axis=0, tiled=True
    ).reshape(slots, -1)
    in_grad, combine_grad = call(
        home_kernel,
        [((tokens, width), BF16), ((top_count, tokens), BF16)],
        [],
        8,
        (2 * tokens * slots * width, 2 * MIB),
        home,
        kept,
        expert_ids.T,
    )
    return (
        in_grad,
        combine_grad.T,
        grad_gate.astype(jnp.bfloat16)[None],
        grad_up.astype(jnp.bfloat16)[None],
        grad_down.astype(jnp.bfloat16)[None],
    )


def solution(mesh):
    fine = Mesh(
        mesh.devices.reshape(2, 4, 2, 4, 4), ("zlo", "y", "core", "zhi", "x")
    )
    tokens = P(("zlo", "y", "core", "zhi", "x"), None)
    hidden = P(("zhi", "x"), ("zlo", "y", "core"), None)
    return jax.shard_map(
        body,
        mesh=fine,
        in_specs=(tokens,) * 5 + (hidden,) * 3,
        out_specs=(tokens,) * 2 + (hidden,) * 3,
        check_vma=False,
    )
```
